32 devices in a mesh: sp: 4 (over x, core), fsdp: 8 (over z, y).
Axes of the slice: x: 2, y: 2, z: 4, core: 2. Of those that a mesh axis runs over, the one named last changes fastest.
Arguments:
- tokens: bfloat16 [8, 1536, 768], P('fsdp', 'sp'), may hold values from -6 to 6
- w_query: bfloat16 [768, 768], P('fsdp'), may hold values from -0.21875 to 0.21875
- w_key: bfloat16 [768, 768], P('fsdp'), may hold values from -0.21875 to 0.21875
- w_value: bfloat16 [768, 768], P('fsdp'), may hold values from -0.21875 to 0.21875
- w_out: bfloat16 [768, 768], P('fsdp'), may hold values from -1.75 to 1.75
- gain_one: bfloat16 [768], P('fsdp'), may hold values from 0.5 to 1.5
- shift_one: bfloat16 [768], P('fsdp'), may hold values from -1 to 1
- w_gate: bfloat16 [768, 3072], P('fsdp'), may hold values from -0.21875 to 0.21875
- w_up: bfloat16 [768, 3072], P('fsdp'), may hold values from -0.21875 to 0.21875
- w_down: bfloat16 [3072, 768], P('fsdp'), may hold values from -0.21875 to 0.21875
- gain_two: bfloat16 [768], P('fsdp'), may hold values from 0.5 to 1.5
- shift_two: bfloat16 [768], P('fsdp'), may hold values from -1 to 1
- slopes: float32 [12], replicated, may hold values from 0.00390625 to 0.7071
- cotangent: bfloat16 [8, 1536, 768], P('fsdp', 'sp'), may hold values from -6 to 6
Outputs:
- output: bfloat16 [8, 1536, 768], P('fsdp', 'sp')
- input_grad: bfloat16 [8, 1536, 768], P('fsdp', 'sp')
- grad_query: float32 [768, 768], P('fsdp')
- grad_key: float32 [768, 768], P('fsdp')
- grad_value: float32 [768, 768], P('fsdp')
- grad_out: float32 [768, 768], P('fsdp')
- grad_gain_one: float32 [768], P('fsdp')
- grad_shift_one: float32 [768], P('fsdp')
- grad_gate: float32 [768, 3072], P('fsdp')
- grad_up: float32 [768, 3072], P('fsdp')
- grad_down: float32 [3072, 768], P('fsdp')
- grad_gain_two: float32 [768], P('fsdp')
- grad_shift_two: float32 [768], P('fsdp')
The draws below stay inside these ranges and needn't reach their ends.
All inputs are finite; a program needn't handle non-finite values.
Results may differ from the reference program's by a relative error of at most 0.018.
Values may be sent and summed in bfloat16 or wider, within the bound.
A program may use at most 192 MiB of HBM per device.

```python
import math
import jax
import jax.numpy as jnp
from jax import lax

D = 768
HEADS = 12
HEAD_DIM = 64
FF = 3072
ROWS = 1536
PIECES = 8
SEQ_LEN = 6144
SEQS = 2


def shard_levels(own_key, extent, pieces, low, top_value):
    factor_of, own = 1.0, jax.random.fold_in(own_key, 6)
    for position, shards_of in pieces:
        steps = jnp.exp(jax.random.uniform(jax.random.fold_in(own, position), (shards_of,), jnp.float32, low / len(pieces), top_value / len(pieces)))
        factor_of = factor_of * jnp.repeat(steps, extent[position] // shards_of).reshape([-1 if axis == position else 1 for axis in range(len(extent))])
    return factor_of


def gaussian(stream_key, dims, width, reach, split=(), kind=jnp.bfloat16):
    entries = jax.random.normal(stream_key, dims, jnp.float32) * width
    if len(split) > 0:
        entries = shard_levels(stream_key, dims, split, -0.22, 0.18) * entries
    return jnp.clip(entries, min=-reach, max=reach).astype(kind)


def setup_inputs(seed: int = 0) -> dict:
    key_list = jax.random.split(jax.random.key(seed), 15)
    tokens = gaussian(key_list[0], (PIECES, ROWS, D), 1.0, 6.0, ((0, 8), (1, 4)))
    w_query = gaussian(key_list[1], (D, D), D ** -0.5, 0.21875, ((0, 8),))
    w_key = gaussian(key_list[2], (D, D), D ** -0.5, 0.21875, ((0, 8),))
    w_value = gaussian(key_list[3], (D, D), D ** -0.5, 0.21875, ((0, 8),))
    w_out = gaussian(key_list[4], (D, D), (D // 64) ** -0.5, 1.75, ((0, 8),))
    gain_one = jnp.clip(1.0 + 0.1 * jax.random.normal(key_list[5], (D,), jnp.float32), 0.5, 1.5).astype(jnp.bfloat16)
    shift_one = gaussian(key_list[6], (D,), 0.2, 1.0, ((0, 8),))
    w_gate = gaussian(key_list[7], (D, FF), D ** -0.5, 0.21875, ((0, 8),))
    w_up = gaussian(key_list[8], (D, FF), D ** -0.5, 0.21875, ((0, 8),))
    w_down = gaussian(key_list[9], (FF, D), (FF // 4) ** -0.5, 0.21875, ((0, 8),))
    gain_two = jnp.clip(1.0 + 0.1 * jax.random.normal(key_list[10], (D,), jnp.float32), 0.5, 1.5).astype(jnp.bfloat16)
    shift_two = gaussian(key_list[11], (D,), 0.2, 1.0, ((0, 8),))
    slopes = jnp.clip(jnp.exp(jax.random.uniform(key_list[12], (HEADS,), jnp.float32, math.log(0.00390625), math.log(0.7071))), 0.00390625, 0.7071)
    cotangent = gaussian(key_list[13], (PIECES, ROWS, D), 1.0, 6.0, ((0, 8), (1, 4)))
    return {"tokens": tokens, "w_query": w_query, "w_key": w_key, "w_value": w_value, "w_out": w_out, "gain_one": gain_one, "shift_one": shift_one, "w_gate": w_gate, "w_up": w_up, "w_down": w_down, "gain_two": gain_two, "shift_two": shift_two, "slopes": slopes, "cotangent": cotangent}


@jax.custom_vjp
def low(v):
    return lax.optimization_barrier(v.astype(jnp.bfloat16)).astype(jnp.float32)

@jax.custom_vjp
def low_back(v):
    return v

def low_keep(v):
    return (low(v), None)

def low_pass(kept, grad):
    return (grad,)

def back_keep(v):
    return (v, None)

def back_low(kept, grad):
    return (low(grad),)
low.defvjp(low_keep, low_pass)
low_back.defvjp(back_keep, back_low)
EPS = 1e-12
HIGH = lax.Precision.HIGHEST

def matmul(left, right):
    return jnp.dot(left, right, precision=HIGH, preferred_element_type=jnp.float32)

def normalize(residual_sum, gain, shift):
    average = lax.optimization_barrier(jnp.mean(residual_sum, axis=-1, keepdims=True))
    centred = residual_sum - average
    spread = lax.optimization_barrier(jnp.mean(centred * centred, axis=-1, keepdims=True))
    return centred * lax.rsqrt(spread + EPS) * gain + shift

def attend(queries, keys, values, slopes):
    length = queries.shape[0]
    block = min(512, length)
    columns = jnp.arange(length, dtype=jnp.float32)

    def one_block(pair):
        block_queries, start = pair
        raw = jnp.einsum('qhe,khe->hqk', block_queries, keys, precision=HIGH)
        places = start + jnp.arange(block, dtype=jnp.float32)
        distance = jnp.abs(places[:, None] - columns[None, :])
        scores = low_back(raw) * 0.125 - slopes[:, None, None] * distance[None]
        weights = low(jax.nn.softmax(scores, axis=-1))
        return jnp.einsum('hqk,khe->qhe', weights, values, precision=HIGH)
    blocks = queries.reshape(length // block, block, HEADS, HEAD_DIM)
    starts = block * jnp.arange(length // block, dtype=jnp.float32)
    result = lax.map(jax.checkpoint(one_block), (blocks, starts))
    return result.reshape(length, HEADS * HEAD_DIM)

def layer(inputs, weights, slopes):
    w_query, w_key, w_value, w_out, gain_one, shift_one, w_gate, w_up, w_down, gain_two, shift_two = weights
    length = inputs.shape[0]
    queries = low_back(low(matmul(inputs, w_query))).reshape(length, HEADS, HEAD_DIM)
    keys = low_back(low(matmul(inputs, w_key))).reshape(length, HEADS, HEAD_DIM)
    values = low_back(low(matmul(inputs, w_value))).reshape(length, HEADS, HEAD_DIM)
    context = low_back(low(attend(queries, keys, values, slopes)))
    attended = low_back(matmul(context, w_out))
    hidden = normalize(inputs + attended, gain_one, shift_one)
    hidden_low = low(hidden)
    gate = low_back(matmul(hidden_low, w_gate))
    upward = low_back(matmul(hidden_low, w_up))
    active = low(jax.nn.gelu(gate, approximate=False) * upward)
    branch = low_back(matmul(active, w_down))
    return normalize(hidden + branch, gain_two, shift_two)

def reference(tokens, w_query, w_key, w_value, w_out, gain_one, shift_one, w_gate, w_up, w_down, gain_two, shift_two, slopes, cotangent):
    params = tuple((weight.astype(jnp.float32) for weight in (w_query, w_key, w_value, w_out, gain_one, shift_one, w_gate, w_up, w_down, gain_two, shift_two)))
    sequences = tokens.astype(jnp.float32).reshape(SEQS, SEQ_LEN, D)
    incoming_all = cotangent.astype(jnp.float32).reshape(SEQS, SEQ_LEN, D)

    def forward(inputs, *weights):
        return layer(inputs, weights, slopes)

    def one_sequence(totals, pair):
        source, incoming = pair
        result, pull = jax.vjp(forward, source, *params)
        grads = pull(incoming)
        summed = tuple((total + grad for total, grad in zip(totals, grads[1:])))
        return (summed, (result, grads[0]))
    zeros = tuple((jnp.zeros(weight.shape, jnp.float32) for weight in params))
    totals, (results, input_grads) = lax.scan(one_sequence, zeros, (sequences, incoming_all))
    output = results.reshape(PIECES, ROWS, D).astype(jnp.bfloat16)
    input_grad = input_grads.reshape(PIECES, ROWS, D).astype(jnp.bfloat16)
    return (output, input_grad, totals[0], totals[1], totals[2], totals[3], totals[4], totals[5], totals[6], totals[7], totals[8], totals[9], totals[10])
```

```python
import functools

import jax
import jax.numpy as jnp
from jax import lax
from jax.experimental import pallas as pl
from jax.experimental.pallas import tpu as pltpu
from jax.sharding import PartitionSpec as P

HEADS = 12
HEAD_DIM = 64
GROUP = 4
VALUE_ROWS = 80
VMEM_BYTES = 50 * 1024 * 1024


EPS = 1e-12


def from_partner(array, axis, distance):
    return lax.ppermute(array, axis, [(i, i ^ distance) for i in range(lax.axis_size(axis))])


def from_sp(array, distance):
    return from_partner(array, "sp", distance)


def normalize(residual_sum, gain, shift):
    average = jnp.mean(residual_sum, axis=-1, keepdims=True)
    centred = residual_sum - average
    spread = jnp.mean(centred * centred, axis=-1, keepdims=True)
    return centred * lax.rsqrt(spread + EPS) * gain + shift


def geglu(gate, upward):
    return jax.nn.gelu(gate, approximate=False) * upward


def product(left, right):
    return jnp.dot(left, right, preferred_element_type=jnp.float32)


def product_left(left, right):
    return lax.dot_general(
        left, right, (((0,), (0,)), ((), ())), preferred_element_type=jnp.float32
    )


def product_right(left, right):
    return lax.dot_general(
        left, right, (((1,), (1,)), ((), ())), preferred_element_type=jnp.float32
    )


def ramp(block):
    shape = (block, block)
    down = lax.broadcasted_iota(jnp.int32, shape, 0)
    across = lax.broadcasted_iota(jnp.int32, shape, 1)
    return (down - across).astype(jnp.float32)


def forward_kernel(block, slopes_ref, bases_ref, q_ref, k_ref, v_ref, o_ref, lse_ref, tile_ref):
    head = pl.program_id(0)
    place = pl.program_id(1)
    slope = slopes_ref[head]

    @pl.when(place == 0)
    def _():
        tile_ref[...] = ramp(block) * slope

    queries = q_ref[0]
    start = bases_ref[place]

    def step(chunk, carry):
        highest, total = carry
        rows = pl.ds(pl.multiple_of(chunk * block, block), block)
        raw = jnp.dot(k_ref[0, rows, :], queries, preferred_element_type=jnp.float32)
        shift = slope * (bases_ref[chunk] - start)
        scores = raw - jnp.abs(tile_ref[...] + shift)
        newest = jnp.maximum(highest, jnp.max(scores, axis=0, keepdims=True))
        raised = jnp.exp(scores - newest).astype(jnp.bfloat16)
        part = jnp.dot(v_ref[0, :, rows], raised, preferred_element_type=jnp.float32)
        return newest, total * jnp.exp(highest - newest) + part

    chunks = k_ref.shape[1] // block
    highest = jnp.full((1, block), -jnp.inf, jnp.float32)
    total = jnp.zeros((VALUE_ROWS, block), jnp.float32)
    highest, total = lax.fori_loop(0, chunks, step, (highest, total), unroll=4)
    sums = total[HEAD_DIM : HEAD_DIM + 1]
    o_ref[0] = total[:HEAD_DIM] / sums
    lse_ref[0] = highest + jnp.log(sums)


def backward_kernel(
    block,
    slopes_ref,
    bases_ref,
    qt_ref,
    q_ref,
    gt_ref,
    g_ref,
    o_ref,
    lse_ref,
    k_ref,
    kt_ref,
    v_ref,
    dq_ref,
    dk_ref,
    dv_ref,
    tile_ref,
):
    head = pl.program_id(0)
    place = pl.program_id(1)
    slope = slopes_ref[head]

    @pl.when(place == 0)
    def _():
        tile_ref[...] = ramp(block) * slope
        dk_ref[...] = jnp.zeros_like(dk_ref)
        dv_ref[...] = jnp.zeros_like(dv_ref)

    start = bases_ref[place]
    queries_t = qt_ref[0]
    grads_t = gt_ref[0]
    logsum = lse_ref[0]
    means = jnp.sum(grads_t.astype(jnp.float32) * o_ref[0], axis=0, keepdims=True)

    def step(chunk, total):
        rows = pl.ds(pl.multiple_of(chunk * block, block), block)
        raw = jnp.dot(k_ref[0, rows, :], queries_t, preferred_element_type=jnp.float32)
        shift = slope * (bases_ref[chunk] - start)
        probs = jnp.exp(raw - jnp.abs(tile_ref[...] + shift) - logsum)
        d_probs = jnp.dot(v_ref[0, rows, :], grads_t, preferred_element_type=jnp.float32)
        d_scores = (probs * (d_probs - means)).astype(jnp.bfloat16)
        dv_ref[0, rows, :] += jnp.dot(
            probs.astype(jnp.bfloat16), g_ref[0], preferred_element_type=jnp.float32
        )
        dk_ref[0, rows, :] += jnp.dot(d_scores, q_ref[0], preferred_element_type=jnp.float32)
        return total + jnp.dot(kt_ref[0, :, rows], d_scores, preferred_element_type=jnp.float32)

    chunks = k_ref.shape[1] // block
    total = jnp.zeros((HEAD_DIM, block), jnp.float32)
    total = lax.fori_loop(0, chunks, step, total, unroll=2)
    dq_ref[0] = total * 0.125


def scalars():
    return pl.BlockSpec(memory_space=pltpu.SMEM)


def across(rows, block):
    return pl.BlockSpec((1, rows, block), lambda h, i: (h, 0, i))


def down(block):
    return pl.BlockSpec((1, block, HEAD_DIM), lambda h, i: (h, i, 0))


def whole(rows, columns):
    return pl.BlockSpec((1, rows, columns), lambda h, i: (h, 0, 0))


def attend_forward(slopes, bases, queries_t, keys, values_t, block):
    heads, width, count = queries_t.shape
    length = keys.shape[1]
    work = heads * count * length
    return pl.pallas_call(
        functools.partial(forward_kernel, block),
        grid=(heads, count // block),
        in_specs=[
            scalars(),
            scalars(),
            across(width, block),
            whole(length, width),
            whole(VALUE_ROWS, length),
        ],
        out_specs=[across(width, block), across(1, block)],
        out_shape=[
            jax.ShapeDtypeStruct((heads, width, count), jnp.float32),
            jax.ShapeDtypeStruct((heads, 1, count), jnp.float32),
        ],
        scratch_shapes=[pltpu.VMEM((block, block), jnp.float32)],
        compiler_params=pltpu.CompilerParams(vmem_limit_bytes=VMEM_BYTES),
        cost_estimate=pl.CostEstimate(
            flops=16 * work * width, bytes_accessed=16 * heads * length * width, transcendentals=work
        ),
    )(slopes, bases, queries_t, keys, values_t)


def attend_backward(
    slopes, bases, queries_t, queries, grads_t, grads, context_t, logsum, keys, keys_t, values, block
):
    heads, width, count = queries_t.shape
    length = keys.shape[1]
    work = heads * count * length
    return pl.pallas_call(
        functools.partial(backward_kernel, block),
        grid=(heads, count // block),
        in_specs=[
            scalars(),
            scalars(),
            across(width, block),
            down(block),
            across(width, block),
            down(block),
            across(width, block),
            across(1, block),
            whole(length, width),
            whole(width, length),
            whole(length, width),
        ],
        out_specs=[across(width, block), whole(length, width), whole(length, width)],
        out_shape=[
            jax.ShapeDtypeStruct((heads, width, count), jnp.float32),
            jax.ShapeDtypeStruct((heads, length, width), jnp.float32),
            jax.ShapeDtypeStruct((heads, length, width), jnp.float32),
        ],
        scratch_shapes=[pltpu.VMEM((block, block), jnp.float32)],
        compiler_params=pltpu.CompilerParams(vmem_limit_bytes=VMEM_BYTES),
        cost_estimate=pl.CostEstimate(
            flops=40 * work * width, bytes_accessed=32 * heads * length * width, transcendentals=work
        ),
    )(slopes, bases, queries_t, queries, grads_t, grads, context_t, logsum, keys, keys_t, values)


def gather_rows(shard):
    return lax.all_gather(shard, "fsdp", axis=0, tiled=True)


def four_from_sp(mine):
    opposite = from_sp(mine, 2)
    return (mine, from_sp(mine, 1), opposite, from_sp(opposite, 1))


def sum_to_quarter(parts):
    low = [part.astype(jnp.bfloat16) for part in parts]
    near = parts[0] + from_sp(low[1], 1).astype(jnp.float32)
    far = parts[2] + from_sp(low[3], 1).astype(jnp.float32)
    return near + from_sp(far.astype(jnp.bfloat16), 2).astype(jnp.float32)


def scatter_rows(quarter):
    low = lax.psum_scatter(
        quarter.astype(jnp.bfloat16), "fsdp", scatter_dimension=0, tiled=True
    )
    return lax.all_gather(low, "sp", axis=0, tiled=False).astype(jnp.float32)


def body(
    tokens,
    w_query,
    w_key,
    w_value,
    w_out,
    gain_one,
    shift_one,
    w_gate,
    w_up,
    w_down,
    gain_two,
    shift_two,
    slopes,
    cotangent,
):
    groups = lax.axis_size("sp")
    owners = lax.axis_size("fsdp")
    me = lax.axis_index("sp")
    source = tokens[0]
    count, width = source.shape
    head_width = HEADS // groups * HEAD_DIM
    local_heads = HEADS // groups
    seq_rows = groups * count
    hidden_units = w_gate.shape[1]
    hidden_part = hidden_units // groups
    piece_part = hidden_part // owners
    bf16 = jnp.bfloat16
    f32 = jnp.float32

    def my_columns(weight):
        return lax.dynamic_slice_in_dim(weight, me * head_width, head_width, axis=1)

    def my_units(weight):
        split = weight.reshape(weight.shape[0], owners, groups, piece_part)
        return lax.dynamic_index_in_dim(split, me, 2, keepdims=False).reshape(-1, hidden_part)

    w_three = gather_rows(
        jnp.concatenate((my_columns(w_query), my_columns(w_key), my_columns(w_value)), axis=1)
    )
    threes = four_from_sp(w_three)
    vectors = jnp.stack((gain_one, shift_one, gain_two, shift_two), axis=1)
    my_down = lax.dynamic_slice_in_dim(w_down, me * piece_part, piece_part, axis=0)
    w_pairs = gather_rows(jnp.concatenate((my_units(w_gate), my_units(w_up)), axis=1))
    w_rest = gather_rows(my_down)
    out_full = gather_rows(w_out)
    vectors_full = gather_rows(vectors).astype(f32)
    gain_a, shift_a, gain_b, shift_b = [vectors_full[:, i] for i in range(4)]
    pair_parts = four_from_sp(w_pairs)
    gate_full = jnp.concatenate([part[:, :hidden_part] for part in pair_parts], axis=1)
    up_full = jnp.concatenate([part[:, hidden_part:] for part in pair_parts], axis=1)
    down_full = jnp.concatenate(four_from_sp(w_rest), axis=0)

    projected = [product(source, weight).astype(bf16) for weight in threes]
    arrived = [projected[0]] + [from_sp(projected[p], p) for p in range(1, groups)]
    arrived = jnp.concatenate(arrived, axis=0)
    member = lax.axis_index("fsdp") % GROUP
    my_slopes = lax.dynamic_slice_in_dim(slopes, me * local_heads, local_heads)
    chunk = jnp.arange(groups, dtype=jnp.int32) ^ me
    piece = jnp.arange(GROUP, dtype=jnp.int32) ^ member
    bases = (piece[:, None] * seq_rows + chunk[None, :] * count).reshape(-1).astype(f32)

    pairs = [arrived[:, head_width:]]
    distance = 1
    while distance < GROUP:
        pairs = pairs + [from_partner(pair, "fsdp", distance) for pair in pairs]
        distance *= 2
    known = jnp.concatenate(pairs, axis=0)

    def by_head(rows):
        return jnp.transpose(rows.reshape(rows.shape[0], local_heads, HEAD_DIM), (1, 0, 2))

    def by_head_t(rows):
        return jnp.transpose(rows.reshape(rows.shape[0], local_heads, HEAD_DIM), (1, 2, 0))

    scaled = arrived[:, :head_width] * jnp.asarray(0.125, bf16)
    queries, queries_t = by_head(scaled), by_head_t(scaled)
    key_rows, value_rows = known[:, :head_width], known[:, head_width:]
    keys, keys_t = by_head(key_rows), by_head_t(key_rows)
    values, values_t = by_head(value_rows), by_head_t(value_rows)
    extra = (local_heads, VALUE_ROWS - HEAD_DIM, values_t.shape[2])
    first = lax.broadcasted_iota(jnp.int32, extra, 1) == 0
    values_t = jnp.concatenate((values_t, first.astype(bf16)), axis=1)
    context_t, logsum = attend_forward(my_slopes, bases, queries_t, keys, values_t, count)

    sending = context_t.astype(bf16).reshape(head_width, groups, count)
    returned = [sending[:, 0]] + [from_sp(sending[:, p], p) for p in range(1, groups)]
    ordered = jnp.take(jnp.stack(returned), chunk, axis=0, mode="clip").reshape(width, count)
    context_rows = jnp.transpose(ordered)
    base = source.astype(f32)
    attended = product(context_rows, out_full)
    hidden, pull_one = jax.vjp(normalize, base + attended, gain_a, shift_a)
    hidden_low = hidden.astype(bf16)
    gate = product(hidden_low, gate_full)
    upward = product(hidden_low, up_full)
    active_full, pull_act = jax.vjp(geglu, gate, upward)
    active = active_full.astype(bf16)
    branch = product(active, down_full)
    result, pull_two = jax.vjp(normalize, hidden + branch, gain_b, shift_b)
    output = result.astype(bf16)[None]
    d_second, d_gain_b, d_shift_b = pull_two(cotangent[0].astype(f32))
    d_branch = d_second.astype(bf16)
    d_active = product_right(d_branch, down_full)
    d_gate, d_upward = pull_act(d_active)
    d_gate = d_gate.astype(bf16)
    d_upward = d_upward.astype(bf16)
    d_hidden = d_second + product_right(d_gate, gate_full) + product_right(d_upward, up_full)
    d_first, d_gain_a, d_shift_a = pull_one(d_hidden)
    d_attended = d_first.astype(bf16)
    d_context = product_right(d_attended, out_full).astype(bf16)

    d_parts = [
        lax.dynamic_slice_in_dim(d_context, (me ^ p) * head_width, head_width, axis=1)
        for p in range(groups)
    ]
    d_heads = [d_parts[0]] + [from_sp(d_parts[p], p) for p in range(1, groups)]
    d_heads = jnp.concatenate(d_heads, axis=0)

    grad_gate = product_left(hidden_low, d_gate)
    grad_up = product_left(hidden_low, d_upward)
    grad_down = product_left(active, d_branch)
    wide = []
    for p in range(groups):
        here = slice(p * hidden_part, (p + 1) * hidden_part)
        attended_part = lax.dynamic_slice_in_dim(
            d_attended, (me ^ p) * head_width, head_width, axis=1
        )
        out_part = product_left(context_rows, attended_part)
        wide.append((grad_gate[:, here], grad_up[:, here], grad_down[here], out_part))
    summed = [sum_to_quarter(parts) for parts in zip(*wide)]
    norm_grads = jnp.stack((d_gain_a, d_shift_a, d_gain_b, d_shift_b), axis=1)
    norm_share = lax.psum(
        lax.psum_scatter(norm_grads, "fsdp", scatter_dimension=0, tiled=True), "sp"
    )

    d_queries_t, d_keys, d_values = attend_backward(
        my_slopes,
        bases,
        queries_t,
        queries,
        by_head_t(d_heads),
        by_head(d_heads),
        context_t,
        logsum,
        keys,
        keys_t,
        values,
        count,
    )

    feed = scatter_rows(jnp.concatenate(summed[:3], axis=1))
    out_share = scatter_rows(summed[3])
    rows_here = w_gate.shape[0]

    def units(shared):
        split = shared.reshape(groups, rows_here, owners, piece_part)
        return jnp.transpose(split, (1, 2, 0, 3)).reshape(rows_here, hidden_units)

    def columns(shared):
        return jnp.transpose(shared, (1, 0, 2)).reshape(rows_here, width)

    pending = jnp.transpose(jnp.concatenate((d_keys, d_values), axis=0), (1, 0, 2))
    pending = pending.reshape(GROUP, seq_rows, 2 * head_width)
    while pending.shape[0] > 1:
        half = pending.shape[0] // 2
        leaving = pending[half:].astype(bf16)
        pending = pending[:half] + from_partner(leaving, "fsdp", half).astype(f32)
    d_queries = jnp.transpose(d_queries_t.reshape(head_width, seq_rows))
    d_all = jnp.concatenate((d_queries.astype(bf16), pending[0].astype(bf16)), axis=1)
    d_all = d_all.reshape(groups, count, 3 * head_width)
    d_rows = [d_all[0]] + [from_sp(d_all[p], p) for p in range(1, groups)]
    grad_threes = [product_left(source, rows) for rows in d_rows]
    d_tokens = d_first
    for rows, weight in zip(d_rows, threes):
        d_tokens = d_tokens + product_right(rows, weight)
    input_grad = d_tokens.astype(bf16)[None]
    three = scatter_rows(sum_to_quarter(grad_threes))
    return (
        output,
        input_grad,
        columns(three[:, :, :head_width]),
        columns(three[:, :, head_width : 2 * head_width]),
        columns(three[:, :, 2 * head_width :]),
        columns(out_share),
        norm_share[:, 0],
        norm_share[:, 1],
        units(feed[:, :, :hidden_part]),
        units(feed[:, :, hidden_part : 2 * hidden_part]),
        feed[:, :, 2 * hidden_part :].reshape(groups * piece_part, width),
        norm_share[:, 2],
        norm_share[:, 3],
    )


def solution(mesh):
    placed = (
        P("fsdp", "sp", None),
        P("fsdp", None),
        P("fsdp", None),
        P("fsdp", None),
        P("fsdp", None),
        P("fsdp"),
        P("fsdp"),
        P("fsdp", None),
        P("fsdp", None),
        P("fsdp", None),
        P("fsdp"),
        P("fsdp"),
        P(),
        P("fsdp", "sp", None),
    )
    return jax.shard_map(
        body,
        mesh=mesh,
        in_specs=placed,
        out_specs=(
            P("fsdp", "sp", None),
            P("fsdp", "sp", None),
            P("fsdp", None),
            P("fsdp", None),
            P("fsdp", None),
            P("fsdp", None),
            P("fsdp"),
            P("fsdp"),
            P("fsdp", None),
            P("fsdp", None),
            P("fsdp", None),
            P("fsdp"),
            P("fsdp"),
        ),
        check_vma=False,
    )
```

```python
import functools

import jax
import jax.numpy as jnp
from jax import lax
from jax.experimental import pallas as pl
from jax.experimental.pallas import tpu as pltpu
from jax.sharding import PartitionSpec as P

HEADS = 12
HEAD_DIM = 64
GROUP = 4
VALUE_ROWS = 80
VMEM_BYTES = 50 * 1024 * 1024


EPS = 1e-12


def from_partner(array, axis, distance):
    return lax.ppermute(array, axis, [(i, i ^ distance) for i in range(lax.axis_size(axis))])


def from_sp(array, distance):
    return from_partner(array, "sp", distance)


def normalize(residual_sum, gain, shift):
    average = jnp.mean(residual_sum, axis=-1, keepdims=True)
    centred = residual_sum - average
    spread = jnp.mean(centred * centred, axis=-1, keepdims=True)
    return centred * lax.rsqrt(spread + EPS) * gain + shift


def geglu(gate, upward):
    return jax.nn.gelu(gate, approximate=False) * upward


def product(left, right):
    return jnp.dot(left, right, preferred_element_type=jnp.float32)


def product_left(left, right):
    return lax.dot_general(
        left, right, (((0,), (0,)), ((), ())), preferred_element_type=jnp.float32
    )


def product_right(left, right):
    return lax.dot_general(
        left, right, (((1,), (1,)), ((), ())), preferred_element_type=jnp.float32
    )


def ramp(block):
    shape = (block, block)
    down = lax.broadcasted_iota(jnp.int32, shape, 0)
    across = lax.broadcasted_iota(jnp.int32, shape, 1)
    return (down - across).astype(jnp.float32)


def forward_kernel(block, slopes_ref, bases_ref, q_ref, k_ref, v_ref, o_ref, lse_ref, tile_ref):
    head = pl.program_id(0)
    place = pl.program_id(1)
    slope = slopes_ref[head]

    @pl.when(place == 0)
    def _():
        tile_ref[...] = ramp(block) * slope

    queries = q_ref[0]
    start = bases_ref[place]

    def step(chunk, carry):
        highest, total = carry
        rows = pl.ds(pl.multiple_of(chunk * block, block), block)
        raw = jnp.dot(k_ref[0, rows, :], queries, preferred_element_type=jnp.float32)
        shift = slope * (bases_ref[chunk] - start)
        scores = raw - jnp.abs(tile_ref[...] + shift)
        newest = jnp.maximum(highest, jnp.max(scores, axis=0, keepdims=True))
        raised = jnp.exp(scores - newest).astype(jnp.bfloat16)
        part = jnp.dot(v_ref[0, :, rows], raised, preferred_element_type=jnp.float32)
        return newest, total * jnp.exp(highest - newest) + part

    chunks = k_ref.shape[1] // block
    highest = jnp.full((1, block), -jnp.inf, jnp.float32)
    total = jnp.zeros((VALUE_ROWS, block), jnp.float32)
    highest, total = lax.fori_loop(0, chunks, step, (highest, total), unroll=4)
    sums = total[HEAD_DIM : HEAD_DIM + 1]
    o_ref[0] = total[:HEAD_DIM] / sums
    lse_ref[0] = highest + jnp.log(sums)


def backward_kernel(
    head,
    block,
    slopes_ref,
    bases_ref,
    qt_ref,
    q_ref,
    gt_ref,
    g_ref,
    o_ref,
    lse_ref,
    k_ref,
    kt_ref,
    v_ref,
    dq_ref,
    pair_ref,
    dk_ref,
    dv_ref,
    tile_ref,
):
    place = pl.program_id(0)
    slope = slopes_ref[head]

    @pl.when(place == 0)
    def _():
        tile_ref[...] = ramp(block) * slope
        dk_ref[...] = jnp.zeros_like(dk_ref)
        dv_ref[...] = jnp.zeros_like(dv_ref)

    start = bases_ref[place]
    queries_t = qt_ref[0]
    grads_t = gt_ref[0]
    logsum = lse_ref[0]
    means = jnp.sum(grads_t.astype(jnp.float32) * o_ref[0], axis=0, keepdims=True)

    def step(chunk, total):
        rows = pl.ds(pl.multiple_of(chunk * block, block), block)
        raw = jnp.dot(k_ref[0, rows, :], queries_t, preferred_element_type=jnp.float32)
        shift = slope * (bases_ref[chunk] - start)
        probs = jnp.exp(raw - jnp.abs(tile_ref[...] + shift) - logsum)
        d_probs = jnp.dot(v_ref[0, rows, :], grads_t, preferred_element_type=jnp.float32)
        d_scores = (probs * (d_probs - means)).astype(jnp.bfloat16)
        dv_ref[rows, :] += jnp.dot(
            probs.astype(jnp.bfloat16), g_ref[0], preferred_element_type=jnp.float32
        )
        dk_ref[rows, :] += jnp.dot(d_scores, q_ref[0], preferred_element_type=jnp.float32)
        return total + jnp.dot(kt_ref[0, :, rows], d_scores, preferred_element_type=jnp.float32)

    chunks = k_ref.shape[1] // block
    total = jnp.zeros((HEAD_DIM, block), jnp.float32)
    total = lax.fori_loop(0, chunks, step, total, unroll=2)
    dq_ref[0] = total * 0.125

    @pl.when(place == pl.num_programs(0) - 1)
    def _():
        pair_ref[...] = jnp.concatenate((dk_ref[...], dv_ref[...]), axis=1).astype(jnp.bfloat16)


def scalars():
    return pl.BlockSpec(memory_space=pltpu.SMEM)


def across(rows, block):
    return pl.BlockSpec((1, rows, block), lambda h, i: (h, 0, i))


def whole(rows, columns):
    return pl.BlockSpec((1, rows, columns), lambda h, i: (h, 0, 0))


def attend_forward(slopes, bases, queries_t, keys, values_t, block):
    heads, width, count = queries_t.shape
    length = keys.shape[1]
    work = heads * count * length
    return pl.pallas_call(
        functools.partial(forward_kernel, block),
        grid=(heads, count // block),
        in_specs=[
            scalars(),
            scalars(),
            across(width, block),
            whole(length, width),
            whole(VALUE_ROWS, length),
        ],
        out_specs=[across(width, block), across(1, block)],
        out_shape=[
            jax.ShapeDtypeStruct((heads, width, count), jnp.float32),
            jax.ShapeDtypeStruct((heads, 1, count), jnp.float32),
        ],
        scratch_shapes=[pltpu.VMEM((block, block), jnp.float32)],
        compiler_params=pltpu.CompilerParams(vmem_limit_bytes=VMEM_BYTES),
        cost_estimate=pl.CostEstimate(
            flops=16 * work * width, bytes_accessed=16 * heads * length * width, transcendentals=work
        ),
    )(slopes, bases, queries_t, keys, values_t)


def attend_backward(
    head, slopes, bases, queries_t, queries, grads_t, grads, context_t, logsum, keys, keys_t, values, block
):
    heads, width, count = queries_t.shape
    length = keys.shape[1]
    work = count * length

    def across_one(rows):
        return pl.BlockSpec((1, rows, block), lambda i: (head, 0, i))

    def whole_one(rows, columns):
        return pl.BlockSpec((1, rows, columns), lambda i: (head, 0, 0))

    down_one = pl.BlockSpec((1, block, width), lambda i: (head, i, 0))
    return pl.pallas_call(
        functools.partial(backward_kernel, head, block),
        grid=(count // block,),
        in_specs=[
            scalars(),
            scalars(),
            across_one(width),
            down_one,
            across_one(width),
            down_one,
            across_one(width),
            across_one(1),
            whole_one(length, width),
            whole_one(width, length),
            whole_one(length, width),
        ],
        out_specs=[
            pl.BlockSpec((1, width, block), lambda i: (0, 0, i)),
            pl.BlockSpec((length, 2 * width), lambda i: (0, 0)),
        ],
        out_shape=[
            jax.ShapeDtypeStruct((1, width, count), jnp.float32),
            jax.ShapeDtypeStruct((length, 2 * width), jnp.bfloat16),
        ],
        scratch_shapes=[
            pltpu.VMEM((length, width), jnp.float32),
            pltpu.VMEM((length, width), jnp.float32),
            pltpu.VMEM((block, block), jnp.float32),
        ],
        compiler_params=pltpu.CompilerParams(vmem_limit_bytes=VMEM_BYTES),
        cost_estimate=pl.CostEstimate(
            flops=40 * work * width, bytes_accessed=32 * length * width, transcendentals=work
        ),
    )(slopes, bases, queries_t, queries, grads_t, grads, context_t, logsum, keys, keys_t, values)


def gather_rows(shard):
    return lax.all_gather(shard, "fsdp", axis=0, tiled=True)


def four_from_sp(mine):
    opposite = from_sp(mine, 2)
    return (mine, from_sp(mine, 1), opposite, from_sp(opposite, 1))


def sum_near(low):
    near = low[0].astype(jnp.float32) + from_sp(low[1], 1).astype(jnp.float32)
    far = low[2].astype(jnp.float32) + from_sp(low[3], 1).astype(jnp.float32)
    return near, far.astype(jnp.bfloat16)


def sum_far(near, far):
    return (near + from_sp(far, 2).astype(jnp.float32)).astype(jnp.bfloat16)


def halve_rows(rows):
    distance = rows.shape[0] // 2
    flips = []
    step = 1
    while step <= distance:
        flips.append(step)
        step *= 2
    kept = [rows[i] for i in range(rows.shape[0])]
    for flip in flips:
        leaving = jnp.concatenate(kept[1::2], axis=0).astype(jnp.bfloat16)
        landed = from_partner(leaving, "fsdp", flip).astype(jnp.float32)
        landed = landed.reshape((len(kept) // 2,) + rows.shape[1:])
        kept = [kept[2 * i] + landed[i] for i in range(len(kept) // 2)]
    return kept[0]


def share_rows(quarter):
    return lax.all_gather(quarter.astype(jnp.bfloat16), "sp", axis=0, tiled=False).astype(jnp.float32)


def body(
    tokens,
    w_query,
    w_key,
    w_value,
    w_out,
    gain_one,
    shift_one,
    w_gate,
    w_up,
    w_down,
    gain_two,
    shift_two,
    slopes,
    cotangent,
):
    groups = lax.axis_size("sp")
    owners = lax.axis_size("fsdp")
    me = lax.axis_index("sp")
    source = tokens[0]
    count, width = source.shape
    head_width = HEADS // groups * HEAD_DIM
    local_heads = HEADS // groups
    seq_rows = groups * count
    hidden_units = w_gate.shape[1]
    hidden_part = hidden_units // groups
    piece_part = hidden_part // owners
    bf16 = jnp.bfloat16
    f32 = jnp.float32

    def my_columns(weight):
        return lax.dynamic_slice_in_dim(weight, me * head_width, head_width, axis=1)

    def my_units(weight):
        split = weight.reshape(weight.shape[0], owners, groups, piece_part)
        return lax.dynamic_index_in_dim(split, me, 2, keepdims=False).reshape(-1, hidden_part)

    w_three = gather_rows(
        jnp.concatenate((my_columns(w_query), my_columns(w_key), my_columns(w_value)), axis=1)
    )
    threes = four_from_sp(w_three)
    vectors = jnp.stack((gain_one, shift_one, gain_two, shift_two), axis=1)
    my_down = lax.dynamic_slice_in_dim(w_down, me * piece_part, piece_part, axis=0)
    w_pairs = gather_rows(jnp.concatenate((my_units(w_gate), my_units(w_up)), axis=1))
    vectors = jnp.pad(vectors, ((0, 0), (0, 128 - vectors.shape[1])))
    w_rest = gather_rows(jnp.concatenate((my_down, w_out, vectors), axis=1))
    out_full = w_rest[:, width : 2 * width]
    vectors_full = w_rest[:, 2 * width :].astype(f32)
    gain_a, shift_a, gain_b, shift_b = [vectors_full[:, i] for i in range(4)]
    pair_parts = four_from_sp(w_pairs)
    gate_full = jnp.concatenate([part[:, :hidden_part] for part in pair_parts], axis=1)
    up_full = jnp.concatenate([part[:, hidden_part:] for part in pair_parts], axis=1)
    down_full = jnp.concatenate(four_from_sp(w_rest[:, :width]), axis=0)

    projected = [product(source, weight).astype(bf16) for weight in threes]
    arrived = [projected[0]] + [from_sp(projected[p], p) for p in range(1, groups)]
    arrived = jnp.concatenate(arrived, axis=0)
    member = lax.axis_index("fsdp") % GROUP
    my_slopes = lax.dynamic_slice_in_dim(slopes, me * local_heads, local_heads)
    chunk = jnp.arange(groups, dtype=jnp.int32) ^ me
    piece = jnp.arange(GROUP, dtype=jnp.int32) ^ member
    bases = (piece[:, None] * seq_rows + chunk[None, :] * count).reshape(-1).astype(f32)

    pairs = [arrived[:, head_width:]]
    distance = 1
    while distance < GROUP:
        pairs = pairs + [from_partner(pair, "fsdp", distance) for pair in pairs]
        distance *= 2
    known = jnp.concatenate(pairs, axis=0)

    def by_head(rows):
        return jnp.transpose(rows.reshape(rows.shape[0], local_heads, HEAD_DIM), (1, 0, 2))

    def by_head_t(rows):
        return jnp.transpose(rows.reshape(rows.shape[0], local_heads, HEAD_DIM), (1, 2, 0))

    scaled = arrived[:, :head_width] * jnp.asarray(0.125, bf16)
    queries, queries_t = by_head(scaled), by_head_t(scaled)
    key_rows, value_rows = known[:, :head_width], known[:, head_width:]
    keys, keys_t = by_head(key_rows), by_head_t(key_rows)
    values, values_t = by_head(value_rows), by_head_t(value_rows)
    extra = (local_heads, VALUE_ROWS - HEAD_DIM, values_t.shape[2])
    first = lax.broadcasted_iota(jnp.int32, extra, 1) == 0
    values_t = jnp.concatenate((values_t, first.astype(bf16)), axis=1)
    context_t, logsum = attend_forward(my_slopes, bases, queries_t, keys, values_t, count)

    sending = context_t.astype(bf16).reshape(head_width, groups, count)
    returned = [sending[:, 0]] + [from_sp(sending[:, p], p) for p in range(1, groups)]
    ordered = jnp.take(jnp.stack(returned), chunk, axis=0, mode="clip").reshape(width, count)
    context_rows = jnp.transpose(ordered)
    base = source.astype(f32)
    attended = product(context_rows, out_full)
    hidden, pull_one = jax.vjp(normalize, base + attended, gain_a, shift_a)
    hidden_low = hidden.astype(bf16)
    gate = product(hidden_low, gate_full)
    upward = product(hidden_low, up_full)
    active_full, pull_act = jax.vjp(geglu, gate, upward)
    active = active_full.astype(bf16)
    branch = product(active, down_full)
    result, pull_two = jax.vjp(normalize, hidden + branch, gain_b, shift_b)
    output = result.astype(bf16)[None]
    d_second, d_gain_b, d_shift_b = pull_two(cotangent[0].astype(f32))
    d_branch = d_second.astype(bf16)
    d_active = product_right(d_branch, down_full)
    d_gate, d_upward = pull_act(d_active)
    d_gate = d_gate.astype(bf16)
    d_upward = d_upward.astype(bf16)
    d_hidden = d_second + product_right(d_gate, gate_full) + product_right(d_upward, up_full)
    d_first, d_gain_a, d_shift_a = pull_one(d_hidden)
    d_attended = d_first.astype(bf16)
    d_context = product_right(d_attended, out_full).astype(bf16)

    d_parts = [
        lax.dynamic_slice_in_dim(d_context, (me ^ p) * head_width, head_width, axis=1)
        for p in range(groups)
    ]
    d_heads = [d_parts[0]] + [from_sp(d_parts[p], p) for p in range(1, groups)]
    d_heads = jnp.concatenate(d_heads, axis=0)

    grad_gate = product_left(hidden_low, d_gate)
    grad_up = product_left(hidden_low, d_upward)
    grad_down = product_left(active, d_branch)
    norm_grads = jnp.stack((d_gain_a, d_shift_a, d_gain_b, d_shift_b), axis=1)
    wide = []
    for p in range(groups):
        here = slice(p * hidden_part, (p + 1) * hidden_part)
        attended_part = lax.dynamic_slice_in_dim(
            d_attended, (me ^ p) * head_width, head_width, axis=1
        )
        out_part = product_left(context_rows, attended_part)
        norm_part = lax.dynamic_slice_in_dim(norm_grads, me ^ p, 1, axis=1)
        side = jnp.concatenate((out_part, jnp.pad(norm_part, ((0, 0), (0, 63)))), axis=1)
        parts = (grad_gate[:, here], grad_up[:, here], grad_down[here], side)
        wide.append(jnp.concatenate([part.astype(bf16) for part in parts], axis=1))
    d_heads_t, d_heads_n = by_head_t(d_heads), by_head(d_heads)
    d_heads_t, d_heads_n, wide = lax.optimization_barrier((d_heads_t, d_heads_n, wide))
    d_head_queries, d_head_pairs = [], []
    held = None
    for head in range(local_heads):
        if head == 1:
            near, far = sum_near(wide)
            d_heads_t, near, far = lax.optimization_barrier((d_heads_t, near, far))
        elif head == 2:
            quarter = sum_far(near, far)
            d_heads_t, quarter = lax.optimization_barrier((d_heads_t, quarter))
        if head:
            d_heads_t, held = lax.optimization_barrier((d_heads_t, held))
            d_head_queries[-1] = held
        held, pair = attend_backward(
            head,
            my_slopes,
            bases,
            queries_t,
            queries,
            d_heads_t,
            d_heads_n,
            context_t,
            logsum,
            keys,
            keys_t,
            values,
            count,
        )
        d_head_queries.append(held)
        d_head_pairs.append(pair)
    feed = share_rows(lax.psum_scatter(quarter, "fsdp", scatter_dimension=0, tiled=True))
    out_share = feed[:, :, 3 * hidden_part : 3 * hidden_part + head_width]
    norm_share = jnp.transpose(feed[:, :, 3 * hidden_part + head_width])
    d_queries_t = jnp.concatenate(d_head_queries, axis=0)

    rows_here = w_gate.shape[0]

    def units(shared):
        split = shared.reshape(groups, rows_here, owners, piece_part)
        return jnp.transpose(split, (1, 2, 0, 3)).reshape(rows_here, hidden_units)

    def columns(shared):
        return jnp.transpose(shared, (1, 0, 2)).reshape(rows_here, width)

    summed_pairs = []
    for pair in d_head_pairs:
        pending = pair.reshape(GROUP, seq_rows, 2 * HEAD_DIM)
        while pending.shape[0] > 1:
            half = pending.shape[0] // 2
            landed = from_partner(pending[half:], "fsdp", half).astype(f32)
            pending = (pending[:half].astype(f32) + landed).astype(bf16)
        summed_pairs.append(pending[0])
    d_pairs = [pair[:, :HEAD_DIM] for pair in summed_pairs]
    d_pairs += [pair[:, HEAD_DIM:] for pair in summed_pairs]
    d_queries = jnp.transpose(d_queries_t.reshape(head_width, seq_rows))
    d_all = jnp.concatenate([d_queries.astype(bf16)] + d_pairs, axis=1)
    d_all = d_all.reshape(groups, count, 3 * head_width)
    d_rows = [d_all[0]] + [from_sp(d_all[p], p) for p in range(1, groups)]
    owner = jnp.arange(owners, dtype=jnp.int32) ^ lax.axis_index("fsdp")
    swapped = jnp.take(source.reshape(count, owners, rows_here), owner, axis=1, mode="clip")
    swapped = swapped.reshape(count, width)
    grad_threes = [product_left(swapped, rows).astype(bf16) for rows in d_rows]
    d_tokens = d_first
    for rows, weight in zip(d_rows, threes):
        d_tokens = d_tokens + product_right(rows, weight)
    input_grad = d_tokens.astype(bf16)[None]
    three = sum_far(*sum_near(grad_threes)).astype(f32)
    three = share_rows(halve_rows(three.reshape(owners, rows_here, 3 * head_width)))
    return (
        output,
        input_grad,
        columns(three[:, :, :head_width]),
        columns(three[:, :, head_width : 2 * head_width]),
        columns(three[:, :, 2 * head_width :]),
        columns(out_share),
        norm_share[:, 0],
        norm_share[:, 1],
        units(feed[:, :, :hidden_part]),
        units(feed[:, :, hidden_part : 2 * hidden_part]),
        feed[:, :, 2 * hidden_part : 3 * hidden_part].reshape(groups * piece_part, width),
        norm_share[:, 2],
        norm_share[:, 3],
    )


def solution(mesh):
    placed = (
        P("fsdp", "sp", None),
        P("fsdp", None),
        P("fsdp", None),
        P("fsdp", None),
        P("fsdp", None),
        P("fsdp"),
        P("fsdp"),
        P("fsdp", None),
        P("fsdp", None),
        P("fsdp", None),
        P("fsdp"),
        P("fsdp"),
        P(),
        P("fsdp", "sp", None),
    )
    return jax.shard_map(
        body,
        mesh=mesh,
        in_specs=placed,
        out_specs=(
            P("fsdp", "sp", None),
            P("fsdp", "sp", None),
            P("fsdp", None),
            P("fsdp", None),
            P("fsdp", None),
            P("fsdp", None),
            P("fsdp"),
            P("fsdp"),
            P("fsdp", None),
            P("fsdp", None),
            P("fsdp", None),
            P("fsdp"),
            P("fsdp"),
        ),
        check_vma=False,
    )
```
